256 devices in a mesh: dp: 64 (over y_hi, z, x), grad: 4 (over y_lo, core).
Axes of the slice: x: 4, y: 4 (y_hi: 2, y_lo: 2; y = y_hi * 2 + y_lo), z: 8, core: 2. Of those that a mesh axis runs over, the one named last changes fastest.
Arguments:
- acts: bfloat16 [2, 32768, 1536], P(None, 'dp'), may hold values from -6 to 6
- prior: bfloat16 [64, 1536, 1536], P('dp', 'grad'), may hold values from -0.05 to 0.6, as said below
- owner: int32 [2], replicated, may hold values from 0 to 63, as said below
- grads: bfloat16 [2, 1536, 6144], P(None, 'grad', 'dp'), may hold values from -6 to 6
Outputs:
- inverse: bfloat16 [2, 1536, 1536], P(None, 'grad')
- precond: bfloat16 [2, 1536, 6144], P(None, 'grad', 'dp')
The draws below stay inside these ranges and needn't reach their ends.
Inputs may be any that keep to these rules, and one draw needn't show every extreme that they name: `owner`: the 2 owners are distinct. `prior`: each slot is symmetric.
All inputs are finite; a program needn't handle non-finite values.
Results may differ from the reference program's by a relative error of at most 0.0053.
Values may be sent and summed in bfloat16 or wider, within the bound.
A program may use at most 64 MiB of HBM per device.

```python
import jax
import jax.numpy as jnp
from jax import lax

D = 1536
FF = 6144
L = 2
ITERS = 2
TOKENS = 32768
N_DP = 64


def draw_prior(key, part):
    key = jax.random.fold_in(key, 11)
    key_diag, key_noise = jax.random.split(key)
    diagonal = jax.random.uniform(key_diag, (N_DP, D), jnp.float32, 0.35, 0.55)
    noise = jax.random.normal(key_noise, (N_DP, D, D), jnp.float32) * (0.03 / D ** 0.5)
    noise = 0.5 * (noise + jnp.swapaxes(noise, 1, 2))
    eye_mask = jnp.eye(D, dtype=jnp.float32)
    whole = noise * (1.0 - eye_mask) + diagonal[:, :, None] * eye_mask
    return whole.astype(jnp.bfloat16)


def draw_owner(key, part):
    key = jax.random.fold_in(key, 23)
    key_rest, key_place = jax.random.split(key)
    others = jax.random.permutation(key_rest, N_DP - 1)[:L - 1].astype(jnp.int32)
    values = jnp.concatenate([jnp.full((1,), N_DP - 1, jnp.int32), others])
    return jax.random.permutation(key_place, values).astype(jnp.int32)


def levels(stream_key, shape, pieces, low, largest):
    level = 1.0
    for position, parts in pieces:
        draws = jax.random.uniform(jax.random.fold_in(jax.random.fold_in(stream_key, 6), position), (parts,), jnp.float32, low / len(pieces), largest / len(pieces))
        level = level * jnp.repeat(jnp.exp(draws), shape[position] // parts).reshape((-1,) + (1,) * (len(shape) - 1 - position))
    return level


def normal_values(rng, shape, spread, most, shards=(), held_as=jnp.bfloat16):
    drawn = spread * jax.random.normal(rng, shape, jnp.float32)
    if shards:
        drawn = drawn * levels(rng, shape, shards, -0.22, 0.18)
    return jnp.clip(drawn, -most, most).astype(held_as)


def setup_inputs(seed: int = 0) -> dict:
    streams_of = jax.random.split(jax.random.key(seed), 5)
    acts = normal_values(streams_of[0], (L, TOKENS, D), 1.0, 6.0, ((1, 64),))
    prior = draw_prior(jax.random.fold_in(streams_of[4], 71), 0)
    owner = draw_owner(jax.random.fold_in(streams_of[4], 71), 0)
    grads = normal_values(streams_of[3], (L, D, FF), 1.0, 6.0, ((1, 4), (2, 64)))
    return {"acts": acts, "prior": prior, "owner": owner, "grads": grads}


damping = 1e-3


def reference(acts, prior, owner, grads):
    inverses = []
    results = []
    for layer_index in range(L):
        layer_acts = acts[layer_index]
        gram_sum = jnp.dot(layer_acts.T, layer_acts, preferred_element_type=jnp.float32)
        factor = (gram_sum / TOKENS + damping * jnp.eye(D, dtype=jnp.float32)).astype(jnp.bfloat16)
        iterate = lax.dynamic_index_in_dim(prior, owner[layer_index].astype(jnp.int32), 0, keepdims=False)
        for sweep_index in range(ITERS):
            product = jnp.dot(factor, iterate, preferred_element_type=jnp.float32).astype(jnp.bfloat16)
            squared = jnp.dot(iterate, product, preferred_element_type=jnp.float32)
            iterate = (2.0 * iterate.astype(jnp.float32) - squared).astype(jnp.bfloat16)
        inverses.append(iterate)
        results.append(jnp.dot(iterate, grads[layer_index], preferred_element_type=jnp.float32).astype(jnp.bfloat16))
    return jnp.stack(inverses), jnp.stack(results)
```

```python
import functools

import jax
import jax.numpy as jnp
from jax import lax
from jax.experimental import pallas as pl
from jax.experimental.pallas import tpu as pltpu
from jax.sharding import PartitionSpec as P

MESH = pl.DeviceIdType.MESH
BF16, F32 = jnp.bfloat16, jnp.float32
DAMPING = 0.001
NX, NY, NZ = 4, 4, 8
B = 128
SEMS = 112


class Copies:
    def __init__(self, send, recv):
        self.send, self.recv, self.count, self.started = send, recv, 0, []

    def start(self, src, dst, device):
        copy = pltpu.make_async_remote_copy(
            src_ref=src,
            dst_ref=dst,
            send_sem=self.send.at[self.count],
            recv_sem=self.recv.at[self.count],
            device_id=device,
            device_id_type=MESH,
        )
        self.count += 1
        copy.start()
        self.started.append(copy)
        return copy

    def finish(self):
        for copy in self.started:
            copy.wait_send()


def add_rows(buf, rows, extras):
    start, size = rows
    tile = 80 if size % 80 == 0 else 64

    @pl.loop(0, size // tile)
    def _(i):
        at = pl.ds(pl.multiple_of(start + i * tile, 16), tile)
        total = buf[at, :].astype(F32)
        for ref, offset in extras:
            total += ref[pl.ds(pl.multiple_of(offset + i * tile, 16), tile), :].astype(F32)
        buf[at, :] = total.astype(BF16)


def ring_reduce(copies, buf, base, shard, n, me, nxt, prv, land):
    half, far = shard // 2, n // 2

    def rows(k):
        return base + lax.rem(me + k + n, n) * shard

    for step in range(far):
        k = far - step
        if step == 0:
            at = rows(far)
            up = copies.start(
                buf.at[pl.ds(pl.multiple_of(at, 16), half)], land.at[0, step, pl.ds(0, half)], nxt
            )
            down = copies.start(
                buf.at[pl.ds(pl.multiple_of(at + half, 16), half)],
                land.at[1, step, pl.ds(0, half)],
                prv,
            )
        else:
            up = copies.start(
                buf.at[pl.ds(pl.multiple_of(rows(k), 16), shard)],
                land.at[0, step, pl.ds(0, shard)],
                nxt,
            )
            down = copies.start(
                buf.at[pl.ds(pl.multiple_of(rows(-k), 16), shard)],
                land.at[1, step, pl.ds(0, shard)],
                prv,
            )
        yield
        up.wait_recv()
        if step == 0:
            add_rows(buf, (rows(k - 1), half), [(land.at[0, step], 0)])
        elif k > 1:
            add_rows(buf, (rows(k - 1), shard), [(land.at[0, step], 0)])
        down.wait_recv()
        if step == 0:
            add_rows(buf, (rows(1 - k) + half, half), [(land.at[1, step], 0)])
        elif k > 1:
            add_rows(buf, (rows(1 - k), shard), [(land.at[1, step], 0)])
    add_rows(buf, (rows(0), shard), [(land.at[0, far - 1], 0), (land.at[1, far - 1], 0)])


def ring_gather(copies, whole, start, size, n, me, nxt, prv):
    far = n // 2

    def part(p, k):
        return whole.at[p, pl.ds(pl.multiple_of(start(lax.rem(me + k + n, n)), 16), size)]

    flying = {}
    for step in range(far):
        for p in range(2):
            for way, device in ((1, nxt), (-1, prv)):
                if step > 0:
                    flying.pop((p, way)).wait_recv()
        for p in range(2):
            for way, device in ((1, nxt), (-1, prv)):
                if step == far - 1 and (way == 1) != (p == 0):
                    continue
                block = part(p, -way * step)
                flying[p, way] = copies.start(block, block, device)
        yield
    for copy in flying.values():
        copy.wait_recv()


def together(*chains):
    chains = list(chains)
    while chains:
        for chain in list(chains):
            if next(chain, chain) is chain:
                chains.remove(chain)


def matmul_tiles(rows, cols, body):
    tm, tn = 768, 512
    tm = min(tm, rows)

    @pl.loop(0, rows // tm)
    def _(i):
        @pl.loop(0, cols // tn)
        def _(j):
            body(pl.multiple_of(i * tm, tm), tm, pl.ds(pl.multiple_of(j * tn, tn), tn))


def kernel(
    owner, acts, prior, grads, inverse, precond,
    acts_v, prior_v, gram_p, prior_p, land_gz, land_gx, land_px, land_pz, land_gy, land_py,
    all_a, all_x, full_a, full_x, prod, iter1, second, inv_v, grads_v, pre_v,
    send, recv, local,
):
    tokens, width = acts.shape[1], acts.shape[2]
    total = tokens * lax.axis_size("dp")
    dp, g = lax.axis_index("dp"), lax.axis_index("grad")
    x, z, yh = lax.rem(dp, NX), lax.rem(dp // NX, NZ), dp // (NX * NZ)
    h, c = g // 2, lax.rem(g, 2)
    y = yh * 2 + h
    sib = 1 - c

    def at(dx=0, dy=0, dz=0, core=c):
        x2 = lax.rem(x + dx + NX, NX)
        y2 = lax.rem(y + dy + NY, NY)
        z2 = lax.rem(z + dz + NZ, NZ)
        return ((y2 // 2) * (NZ * NX) + z2 * NX + x2, lax.rem(y2, 2) * 2 + core)

    xn, xp, zn, zp = at(dx=1), at(dx=-1), at(dz=1), at(dz=-1)
    ys = [at(dy=1), at(dy=2), at(dy=3)]
    sibling = at(core=sib)
    partner, across = (dp, (1 - h) * 2 + c), (dp, (1 - h) * 2 + sib)
    rows = prior.shape[1]

    loads = [
        pltpu.make_async_copy(prior.at[0], prior_v.at[pl.ds(pl.multiple_of(c * rows, 16), rows)], local.at[0]),
        pltpu.make_async_copy(acts.at[c], acts_v.at[:, pl.ds(0, width)], local.at[1]),
        pltpu.make_async_copy(
            acts.at[c, :, pl.ds(0, width // 2)], acts_v.at[:, pl.ds(width, width // 2)], local.at[2]
        ),
        pltpu.make_async_copy(
            grads.at[c], grads_v.at[pl.ds(pl.multiple_of(g * rows, 16), rows)], local.at[3]
        ),
    ]
    for load in loads:
        load.start()

    barrier = pltpu.get_barrier_semaphore()
    peers = [xn, xp, zn, zp, *ys, sibling, across]
    for peer in peers:
        pl.semaphore_signal(barrier, inc=1, device_id=peer, device_id_type=MESH)
    pl.semaphore_wait(barrier, len(peers))

    copies = Copies(send, recv)
    mine = pl.ds(pl.multiple_of(c * rows, 16), rows)
    swap = copies.start(prior.at[0], prior_v.at[mine], sibling)
    place = pl.ds(pl.multiple_of(g * rows, 16), rows)
    grad_copies = [
        copies.start(grads.at[sib], grads_v.at[place], sibling),
        copies.start(grads.at[c], grads_v.at[place], partner),
        copies.start(grads.at[sib], grads_v.at[place], across),
    ]

    for load in loads:
        load.wait()

    def block_rows(p):
        return pl.ds(pl.multiple_of(p * B, B), B)

    dims = (((0,), (0,)), ((), ()))

    @pl.loop(0, 6)
    def _(ii):
        i = 6 * h + ii
        left = acts_v[:, pl.ds(pl.multiple_of(i * B, B), B)]
        right = acts_v[:, pl.ds(pl.multiple_of(i * B, B), 6 * B)]
        part = lax.dot_general(left, right, dims, preferred_element_type=F32).astype(BF16)
        for d in range(6):
            gram_p[block_rows(ii * 6 + d), :] = part[:, d * B : (d + 1) * B]

    @pl.loop(0, 3)
    def _(e):
        i = 9 * h + e
        j = lax.rem(i + 6, 12)
        left = acts_v[:, pl.ds(pl.multiple_of(i * B, B), B)]
        right = acts_v[:, pl.ds(pl.multiple_of(j * B, B), B)]
        part = lax.dot_general(left, right, dims, preferred_element_type=F32).astype(BF16)
        gram_p[block_rows(36 + e), :] = part

    gram_p[block_rows(39), :] = jnp.zeros((B, B), BF16)

    def reduce_gram():
        yield from ring_reduce(copies, gram_p, 0, 640, NZ, z, zn, zp, land_gz)
        base = z * 640
        yield from ring_reduce(copies, gram_p, base, 160, NX, x, xn, xp, land_gx)
        base = base + x * 160
        other = pl.ds(pl.multiple_of(base + (1 - yh) * 80, 16), 80)
        last = copies.start(gram_p.at[other], land_gy, ys[1])
        yield
        last.wait_recv()
        own = pl.multiple_of(base + yh * 80, 16)
        summed = gram_p[pl.ds(own, 80), :].astype(F32) + land_gy[...].astype(F32)
        at_row = own + lax.broadcasted_iota(jnp.int32, (80, B), 0)
        lane = lax.broadcasted_iota(jnp.int32, (80, B), 1)
        on_diag = lane == at_row
        for p in range(6, 36, 6):
            on_diag = on_diag | (lane + p * B == at_row)
        value = summed / total
        value = jnp.where(on_diag, value + DAMPING, value)
        all_a[h, pl.ds(own, 80), :] = value.astype(BF16)

    def reduce_prior():
        yield from ring_reduce(copies, prior_p, 0, 1280, NX, x, xn, xp, land_px)
        base = x * 1280
        yield from ring_reduce(copies, prior_p, base, 160, NZ, z, zn, zp, land_pz)
        base = base + z * 160
        other = pl.ds(pl.multiple_of(base + (1 - yh) * 80, 16), 80)
        last = copies.start(prior_p.at[other], land_py, ys[1])
        yield
        last.wait_recv()
        own = pl.multiple_of(base + yh * 80, 16)
        summed = prior_p[pl.ds(own, 80), :].astype(F32) + land_py[...].astype(F32)
        all_x[h, pl.ds(own, 80), :] = summed.astype(BF16)

    def gather_y(whole, base):
        own = whole.at[h, pl.ds(pl.multiple_of(base + yh * 80, 16), 80)]
        flying = [copies.start(own, own, device) for device in ys]
        yield
        for copy in flying:
            copy.wait_recv()

    def gather_a():
        yield from gather_y(all_a, (z * NX + x) * 160)
        yield from ring_gather(
            copies, all_a, lambda k: (z * NX + k) * 160, 160, NX, x, xn, xp
        )
        yield from ring_gather(copies, all_a, lambda k: k * 640, 640, NZ, z, zn, zp)

    def gather_x():
        yield from gather_y(all_x, (x * NZ + z) * 160)
        yield from ring_gather(
            copies, all_x, lambda k: (x * NZ + k) * 160, 160, NZ, z, zn, zp
        )
        yield from ring_gather(copies, all_x, lambda k: k * 1280, 1280, NX, x, xn, xp)

    def gram_chain():
        yield from reduce_gram()
        yield from gather_a()

    def prior_chain():
        swap.wait_recv()
        keep = jnp.where(owner[c] == dp, 1.0, 0.0).astype(F32)

        def pack(p, i, j):
            block = prior_v[
                pl.ds(pl.multiple_of((i - 6 * h) * B, B), B), pl.ds(pl.multiple_of(j * B, B), B)
            ]
            prior_p[block_rows(p), :] = (block.astype(F32) * keep).astype(BF16)

        @pl.loop(0, 6)
        def _(ii):
            for d in range(6):
                i = 6 * h + ii
                pack(ii * 6 + d, i, lax.rem(i + d, 12))

        @pl.loop(0, 3)
        def _(e):
            i = 9 * h + e
            pack(36 + e, i, lax.rem(i + 6, 12))

        prior_p[block_rows(39), :] = jnp.zeros((B, B), BF16)
        yield from reduce_prior()
        yield from gather_x()

    together(gram_chain(), prior_chain())

    def unpack(packed, full):
        @pl.loop(0, 12)
        def _(i):
            half, ii = i // 6, lax.rem(i, 6)
            for d in range(6):
                block = packed[half, block_rows(ii * 6 + d), :]
                j = lax.rem(i + d, 12)
                full[block_rows(i), block_rows(j)] = block
                if d:
                    full[block_rows(j), block_rows(i)] = block.T

        @pl.loop(0, 6)
        def _(k):
            half, e = k // 3, lax.rem(k, 3)
            i = 9 * half + e
            j = lax.rem(i + 6, 12)
            block = packed[half, block_rows(36 + e), :]
            full[block_rows(i), block_rows(j)] = block
            full[block_rows(j), block_rows(i)] = block.T

    unpack(all_a, full_a)
    unpack(all_x, full_x)

    def first_product(r, tm, cols):
        at_rows = pl.ds(r, tm)
        prod[at_rows, cols] = jnp.dot(
            full_a[at_rows, :], full_x[:, cols], preferred_element_type=F32
        ).astype(BF16)

    def first_iterate(r, tm, cols):
        at_rows = pl.ds(r, tm)
        squared = jnp.dot(full_x[at_rows, :], prod[:, cols], preferred_element_type=F32)
        iter1[at_rows, cols] = (2.0 * full_x[at_rows, cols].astype(F32) - squared).astype(BF16)

    matmul_tiles(width, width, first_product)
    matmul_tiles(width, width, first_iterate)

    first_row = h * 2 * rows

    def second_product(r, tm, cols):
        source = iter1[pl.ds(pl.multiple_of(first_row + r, 16), tm), :]
        second[pl.ds(r, tm), cols] = jnp.dot(
            source, full_a[:, cols], preferred_element_type=F32
        ).astype(BF16)

    def second_iterate(r, tm, cols):
        squared = jnp.dot(second[pl.ds(r, tm), :], iter1[:, cols], preferred_element_type=F32)
        old = iter1[pl.ds(pl.multiple_of(first_row + r, 16), tm), cols].astype(F32)
        inv_v[pl.ds(r, tm), cols] = (2.0 * old - squared).astype(BF16)

    matmul_tiles(2 * rows, width, second_product)
    matmul_tiles(2 * rows, width, second_iterate)

    for copy in grad_copies:
        copy.wait_recv()
    pre_v[...] = jnp.dot(inv_v[...], grads_v[...], preferred_element_type=F32).astype(BF16)

    theirs = pl.ds(pl.multiple_of(sib * rows, 16), rows)
    results = [
        copies.start(inv_v.at[theirs], inverse.at[c], sibling),
        copies.start(pre_v.at[theirs], precond.at[c], sibling),
    ]
    stores = [
        pltpu.make_async_copy(inv_v.at[mine], inverse.at[c], local.at[0]),
        pltpu.make_async_copy(pre_v.at[mine], precond.at[c], local.at[1]),
    ]
    for store in stores:
        store.start()
    for store in stores:
        store.wait()
    for copy in results:
        copy.wait_recv()
    copies.finish()


def on_device(acts, prior, owner, grads):
    layers, tokens, width = acts.shape
    rows, cols = prior.shape[1], grads.shape[2]
    anywhere = pl.BlockSpec(memory_space=pl.ANY)
    packed = 40 * B
    scratch = [
        pltpu.VMEM((tokens, width + width // 2), BF16),
        pltpu.VMEM((2 * rows, width), BF16),
        pltpu.VMEM((packed, B), BF16),
        pltpu.VMEM((packed, B), BF16),
        pltpu.VMEM((2, 4, 640, B), BF16),
        pltpu.VMEM((2, 2, 160, B), BF16),
        pltpu.VMEM((2, 2, 1280, B), BF16),
        pltpu.VMEM((2, 4, 160, B), BF16),
        pltpu.VMEM((80, B), BF16),
        pltpu.VMEM((80, B), BF16),
        pltpu.VMEM((2, packed, B), BF16),
        pltpu.VMEM((2, packed, B), BF16),
        pltpu.VMEM((width, width), BF16),
        pltpu.VMEM((width, width), BF16),
        pltpu.VMEM((width, width), BF16),
        pltpu.VMEM((width, width), BF16),
        pltpu.VMEM((2 * rows, width), BF16),
        pltpu.VMEM((2 * rows, width), BF16),
        pltpu.VMEM((4 * rows, cols), BF16),
        pltpu.VMEM((2 * rows, cols), BF16),
        pltpu.SemaphoreType.DMA((SEMS,)),
        pltpu.SemaphoreType.DMA((SEMS,)),
        pltpu.SemaphoreType.DMA((4,)),
    ]
    return pl.pallas_call(
        kernel,
        out_shape=(
            jax.ShapeDtypeStruct((layers, rows, width), BF16),
            jax.ShapeDtypeStruct((layers, rows, cols), BF16),
        ),
        in_specs=[pl.BlockSpec(memory_space=pltpu.SMEM), anywhere, anywhere, anywhere],
        out_specs=(anywhere, anywhere),
        scratch_shapes=scratch,
        compiler_params=pltpu.CompilerParams(
            collective_id=0, has_side_effects=True, vmem_limit_bytes=60 * 2**20
        ),
        name="refresh",
    )(owner, acts, prior, grads)


def solution(mesh):
    placed = (P(None, "dp", None), P("dp", "grad", None), P(), P(None, "grad", "dp"))
    return jax.shard_map(
        on_device,
        mesh=mesh,
        in_specs=placed,
        out_specs=(P(None, "grad", None), P(None, "grad", "dp")),
        check_vma=False,
    )
```

```python
import functools

import jax
import jax.numpy as jnp
from jax import lax
from jax.experimental import pallas as pl
from jax.experimental.pallas import tpu as pltpu
from jax.sharding import PartitionSpec as P

MESH = pl.DeviceIdType.MESH
BF16, F32 = jnp.bfloat16, jnp.float32
DAMPING = 0.001
NX, NY, NZ = 4, 4, 8
B = 128
SEMS = 128
CUT = 48


class Copies:
    def __init__(self, send, recv):
        self.send, self.recv, self.count, self.started = send, recv, 0, []

    def start(self, src, dst, device):
        copy = pltpu.make_async_remote_copy(
            src_ref=src,
            dst_ref=dst,
            send_sem=self.send.at[self.count],
            recv_sem=self.recv.at[self.count],
            device_id=device,
            device_id_type=MESH,
        )
        self.count += 1
        copy.start()
        self.started.append(copy)
        return copy

    def finish(self):
        for copy in self.started:
            copy.wait_send()


def add_rows(buf, rows, extras):
    start, size = rows
    tile = 80 if size % 80 == 0 else 64

    @pl.loop(0, size // tile)
    def _(i):
        at = pl.ds(pl.multiple_of(start + i * tile, 16), tile)
        total = buf[at, :].astype(F32)
        for ref, offset in extras:
            total += ref[pl.ds(pl.multiple_of(offset + i * tile, 16), tile), :].astype(F32)
        buf[at, :] = total.astype(BF16)


def ring_reduce(copies, buf, base, shard, n, me, nxt, prv, land):
    half, far = shard // 2, n // 2
    ways = ((0, 1, nxt), (1, -1, prv))

    def row(k, q):
        return base + lax.rem(me + k + n, n) * shard + q * half

    flying = {}
    for step in range(far + 1):
        k = far - step
        order = [(way, q) for q in (0, 1) for way in (0, 1)]
        order = sorted(order, key=lambda wq: wq[0] != wq[1])
        if k == 0:
            for q in (0, 1):
                for way in (0, 1):
                    flying.pop((way, q)).wait_recv()
                add_rows(buf, (row(0, q), half), [(land.at[way, far - 1], q * half) for way in (0, 1)])
            return
        for way, q in order:
            _, sign, device = ways[way]
            old = flying.pop((way, q), None)
            if old is not None:
                old.wait_recv()
                add_rows(buf, (row(sign * k, q), half), [(land.at[way, step - 1], q * half)])
            if step == 0 and way != q:
                continue
            flying[way, q] = copies.start(
                buf.at[pl.ds(pl.multiple_of(row(sign * k, q), 16), half)],
                land.at[way, step, pl.ds(q * half, half)],
                device,
            )
        yield


def direct_reduce(copies, buf, row, peers, land):
    flying = []
    for slot, (where, device) in enumerate(peers):
        source = buf.at[pl.ds(pl.multiple_of(row(*where), 16), 80)]
        flying.append(copies.start(source, land.at[slot], device))
    yield
    total = buf[pl.ds(pl.multiple_of(row(0, 0), 16), 80), :].astype(F32)
    for slot, copy in enumerate(flying):
        copy.wait_recv()
        total += land[slot].astype(F32)
    return total


def direct_gather(copies, block, devices):
    flying = [copies.start(block, block, device) for device in devices]
    yield
    for copy in flying:
        copy.wait_recv()


def ring_gather(copies, part, n, me, nxt, prv):
    far = n // 2
    ways = ((0, 1, nxt), (1, -1, prv))
    flying = {}
    for step in range(far + 1):
        order = [(way, p) for p in (0, 1) for way in (0, 1)]
        order = sorted(order, key=lambda wp: wp[0] != wp[1])
        for way, p in order:
            _, sign, device = ways[way]
            old = flying.pop((way, p), None)
            if old is not None:
                old.wait_recv()
            if step == far or (step == far - 1 and way != p):
                continue
            block = part(p, lax.rem(me - sign * step + n, n))
            flying[way, p] = copies.start(block, block, device)
        if step < far:
            yield


def together(*chains):
    chains = list(chains)
    while chains:
        for chain in list(chains):
            if next(chain, chain) is chain:
                chains.remove(chain)


def matmul_tiles(rows, cols, body):
    tm, tn = 768, 512
    tm = min(tm, rows)

    @pl.loop(0, rows // tm)
    def _(i):
        @pl.loop(0, cols // tn)
        def _(j):
            body(pl.multiple_of(i * tm, tm), tm, pl.ds(pl.multiple_of(j * tn, tn), tn))


def kernel(
    owner, acts, prior, grads, inverse, precond,
    acts_v, prior_v, gram_p, prior_p, land_gz, land_g, land_px, land_p,
    all_a, all_x, full_a, full_x, prod, iter1, second, inv_v, grads_v, pre_v,
    send, recv, local,
):
    tokens, width = acts.shape[1], acts.shape[2]
    total = tokens * lax.axis_size("dp")
    dp, g = lax.axis_index("dp"), lax.axis_index("grad")
    x, z, yh = lax.rem(dp, NX), lax.rem(dp // NX, NZ), dp // (NX * NZ)
    h, c = g // 2, lax.rem(g, 2)
    y = yh * 2 + h
    sib = 1 - c

    def at(dx=0, dy=0, dz=0, core=c):
        x2 = lax.rem(x + dx + NX, NX)
        y2 = lax.rem(y + dy + NY, NY)
        z2 = lax.rem(z + dz + NZ, NZ)
        return ((y2 // 2) * (NZ * NX) + z2 * NX + x2, lax.rem(y2, 2) * 2 + core)

    xn, xp, zn, zp = at(dx=1), at(dx=-1), at(dz=1), at(dz=-1)
    yn, yp = at(dy=1), at(dy=-1)
    xs = [at(dx=k) for k in range(1, NX)]
    ys = [at(dy=k) for k in range(1, NY)]
    zs = [at(dz=k) for k in range(1, NZ)]
    xys = [at(dx=i, dy=j) for i in range(NX) for j in range(NY) if i or j]
    gram_peers = [((i, j), at(dx=i, dy=2 * j)) for i in range(NX) for j in range(2) if i or j]
    prior_peers = [((i, j), at(dz=i, dy=2 * j)) for i in range(NZ) for j in range(2) if i or j]
    sibling = at(core=sib)
    partner, across = (dp, (1 - h) * 2 + c), (dp, (1 - h) * 2 + sib)
    rows = prior.shape[1]

    loads = [
        pltpu.make_async_copy(prior.at[0], prior_v.at[pl.ds(pl.multiple_of(c * rows, 16), rows)], local.at[0]),
        pltpu.make_async_copy(acts.at[c], acts_v.at[:, pl.ds(0, width)], local.at[1]),
        pltpu.make_async_copy(
            acts.at[c, :, pl.ds(0, width // 2)], acts_v.at[:, pl.ds(width, width // 2)], local.at[2]
        ),
        pltpu.make_async_copy(
            grads.at[c], grads_v.at[:, pl.ds(pl.multiple_of(g * rows, 128), rows)], local.at[3]
        ),
    ]
    for load in loads:
        load.start()

    barrier = pltpu.get_barrier_semaphore()
    peers = [*xys, *zs, *[at(dz=i, dy=2) for i in range(1, NZ)], sibling, across]
    for peer in peers:
        pl.semaphore_signal(barrier, inc=1, device_id=peer, device_id_type=MESH)
    pl.semaphore_wait(barrier, len(peers))

    copies = Copies(send, recv)
    mine = pl.ds(pl.multiple_of(c * rows, 16), rows)
    swap = copies.start(prior.at[0], prior_v.at[mine], sibling)
    place = pl.ds(pl.multiple_of(g * rows, 128), rows)
    grad_copies = [
        copies.start(grads.at[sib], grads_v.at[:, place], sibling),
        copies.start(grads.at[c], grads_v.at[:, place], partner),
        copies.start(grads.at[sib], grads_v.at[:, place], across),
    ]

    for load in loads:
        load.wait()

    def block_rows(p):
        return pl.ds(pl.multiple_of(p * B, B), B)

    dims = (((0,), (0,)), ((), ()))

    @pl.loop(0, 6)
    def _(ii):
        i = 6 * h + ii
        left = acts_v[:, pl.ds(pl.multiple_of(i * B, B), B)]
        right = acts_v[:, pl.ds(pl.multiple_of(i * B, B), 6 * B)]
        part = lax.dot_general(left, right, dims, preferred_element_type=F32).astype(BF16)
        for d in range(6):
            gram_p[block_rows(ii * 6 + d), :] = part[:, d * B : (d + 1) * B]

    @pl.loop(0, 3)
    def _(e):
        i = 9 * h + e
        j = lax.rem(i + 6, 12)
        left = acts_v[:, pl.ds(pl.multiple_of(i * B, B), B)]
        right = acts_v[:, pl.ds(pl.multiple_of(j * B, B), B)]
        part = lax.dot_general(left, right, dims, preferred_element_type=F32).astype(BF16)
        gram_p[block_rows(36 + e), :] = part

    gram_p[block_rows(39), :] = jnp.zeros((B, B), BF16)

    def reduce_gram():
        yield from ring_reduce(copies, gram_p, 0, 640, NZ, z, zn, zp, land_gz)

        def row(i, j):
            return z * 640 + lax.rem(x + i, NX) * 160 + lax.rem(yh + j, 2) * 80

        summed = yield from direct_reduce(copies, gram_p, row, gram_peers, land_g)
        at_row = row(0, 0) + lax.broadcasted_iota(jnp.int32, (80, B), 0)
        lane = lax.broadcasted_iota(jnp.int32, (80, B), 1)
        on_diag = lane == at_row
        for p in range(6, 36, 6):
            on_diag = on_diag | (lane + p * B == at_row)
        value = summed / total
        value = jnp.where(on_diag, value + DAMPING, value)
        all_a[h, z, x, yh] = value.astype(BF16)

    def reduce_prior():
        yield from ring_reduce(copies, prior_p, 0, 1280, NX, x, xn, xp, land_px)

        def row(i, j):
            return x * 1280 + lax.rem(z + i, NZ) * 160 + lax.rem(yh + j, 2) * 80

        summed = yield from direct_reduce(copies, prior_p, row, prior_peers, land_p)
        all_x[h, x, z, yh] = summed.astype(BF16)

    first, rest = pl.ds(0, CUT), pl.ds(CUT, 80 - CUT)

    def gather_a_z():
        yield from direct_gather(copies, all_a.at[h, z, x, yh, first], xys)
        yield from ring_gather(
            copies, lambda p, k: all_a.at[p, k, :, :, first], NZ, z, zn, zp
        )

    def gather_a_y():
        yield from direct_gather(copies, all_a.at[h, z, x, yh, rest], zs)
        yield from direct_gather(copies, all_a.at[h, :, x, yh, rest], xs)
        yield from ring_gather(
            copies,
            lambda p, k: all_a.at[lax.rem(k, 2), pl.ds(p * 4, 4), :, k // 2, rest],
            NY, y, yn, yp,
        )

    def gather_x_x():
        yield from direct_gather(copies, all_x.at[h, x, z, yh, first], zs)
        yield from direct_gather(copies, all_x.at[h, x, :, yh, first], ys)
        yield from ring_gather(
            copies, lambda p, k: all_x.at[p, k, :, :, first], NX, x, xn, xp
        )

    def gather_x_y():
        yield from direct_gather(copies, all_x.at[h, x, z, yh, rest], zs)
        yield from direct_gather(copies, all_x.at[h, x, :, yh, rest], xs)
        yield from ring_gather(
            copies,
            lambda p, k: all_x.at[lax.rem(k, 2), :, pl.ds(p * 4, 4), k // 2, rest],
            NY, y, yn, yp,
        )

    def prior_chain():
        swap.wait_recv()
        keep = jnp.where(owner[c] == dp, 1.0, 0.0).astype(F32)

        def pack(p, i, j):
            block = prior_v[
                pl.ds(pl.multiple_of((i - 6 * h) * B, B), B), pl.ds(pl.multiple_of(j * B, B), B)
            ]
            prior_p[block_rows(p), :] = (block.astype(F32) * keep).astype(BF16)

        @pl.loop(0, 6)
        def _(ii):
            for d in range(6):
                i = 6 * h + ii
                pack(ii * 6 + d, i, lax.rem(i + d, 12))

        @pl.loop(0, 3)
        def _(e):
            i = 9 * h + e
            pack(36 + e, i, lax.rem(i + 6, 12))

        prior_p[block_rows(39), :] = jnp.zeros((B, B), BF16)
        yield from reduce_prior()

    together(reduce_gram(), prior_chain())
    together(gather_a_z(), gather_x_x(), gather_a_y(), gather_x_y())

    def unpack(packed, full, groups):
        @pl.loop(0, 2)
        def _(half):
            for group in range(groups):
                size = 40 // groups
                value = packed[half, group].reshape(size * B, B)
                for b in range(size):
                    p = group * size + b
                    if p == 39:
                        continue
                    i, d = (6 * half + p // 6, p % 6) if p < 36 else (9 * half + p - 36, 6)
                    j = lax.rem(i + d, 12)
                    block = value[b * B : (b + 1) * B]
                    full[block_rows(i), block_rows(j)] = block
                    if d:
                        full[block_rows(j), block_rows(i)] = block.T

    unpack(all_a, full_a, NZ)
    unpack(all_x, full_x, NX)

    def first_product(r, tm, cols):
        at_rows = pl.ds(r, tm)
        prod[at_rows, cols] = jnp.dot(
            full_a[at_rows, :], full_x[:, cols], preferred_element_type=F32
        ).astype(BF16)

    def first_iterate(r, tm, cols):
        at_rows = pl.ds(r, tm)
        squared = jnp.dot(full_x[at_rows, :], prod[:, cols], preferred_element_type=F32)
        iter1[at_rows, cols] = (2.0 * full_x[at_rows, cols].astype(F32) - squared).astype(BF16)

    matmul_tiles(width, width, first_product)
    matmul_tiles(width, width, first_iterate)

    first_row = h * 2 * rows

    def second_product(r, tm, cols):
        source = iter1[pl.ds(pl.multiple_of(first_row + r, 16), tm), :]
        second[pl.ds(r, tm), cols] = jnp.dot(
            source, full_a[:, cols], preferred_element_type=F32
        ).astype(BF16)

    def second_iterate(r, tm, cols):
        squared = jnp.dot(second[pl.ds(r, tm), :], iter1[:, cols], preferred_element_type=F32)
        old = iter1[pl.ds(pl.multiple_of(first_row + r, 16), tm), cols].astype(F32)
        inv_v[pl.ds(r, tm), cols] = (2.0 * old - squared).astype(BF16)

    matmul_tiles(2 * rows, width, second_product)
    matmul_tiles(2 * rows, width, second_iterate)

    for copy in grad_copies:
        copy.wait_recv()
    pre_v[...] = lax.dot_general(
        grads_v[...], inv_v[...], (((1,), (1,)), ((), ())), preferred_element_type=F32
    ).astype(BF16)

    theirs = pl.ds(pl.multiple_of(sib * rows, 16), rows)
    their_cols = pl.ds(pl.multiple_of(sib * rows, 128), rows)
    my_cols = pl.ds(pl.multiple_of(c * rows, 128), rows)
    results = [
        copies.start(inv_v.at[theirs], inverse.at[c], sibling),
        copies.start(pre_v.at[:, their_cols], precond.at[c], sibling),
    ]
    stores = [
        pltpu.make_async_copy(inv_v.at[mine], inverse.at[c], local.at[0]),
        pltpu.make_async_copy(pre_v.at[:, my_cols], precond.at[c], local.at[1]),
    ]
    for store in stores:
        store.start()
    for store in stores:
        store.wait()
    for copy in results:
        copy.wait_recv()
    copies.finish()


def on_device(acts, prior, owner, grads):
    layers, tokens, width = acts.shape
    rows, cols = prior.shape[1], grads.shape[2]
    grads = jnp.swapaxes(grads, 1, 2)
    anywhere = pl.BlockSpec(memory_space=pl.ANY)
    packed = 40 * B
    scratch = [
        pltpu.VMEM((tokens, width + width // 2), BF16),
        pltpu.VMEM((2 * rows, width), BF16),
        pltpu.VMEM((packed, B), BF16),
        pltpu.VMEM((packed, B), BF16),
        pltpu.VMEM((2, 4, 640, B), BF16),
        pltpu.VMEM((7, 80, B), BF16),
        pltpu.VMEM((2, 2, 1280, B), BF16),
        pltpu.VMEM((15, 80, B), BF16),
        pltpu.VMEM((2, NZ, NX, 2, 80, B), BF16),
        pltpu.VMEM((2, NX, NZ, 2, 80, B), BF16),
        pltpu.VMEM((width, width), BF16),
        pltpu.VMEM((width, width), BF16),
        pltpu.VMEM((width, width), BF16),
        pltpu.VMEM((width, width), BF16),
        pltpu.VMEM((2 * rows, width), BF16),
        pltpu.VMEM((2 * rows, width), BF16),
        pltpu.VMEM((cols, 4 * rows), BF16),
        pltpu.VMEM((cols, 2 * rows), BF16),
        pltpu.SemaphoreType.DMA((SEMS,)),
        pltpu.SemaphoreType.DMA((SEMS,)),
        pltpu.SemaphoreType.DMA((4,)),
    ]
    inverse, precond = pl.pallas_call(
        kernel,
        out_shape=(
            jax.ShapeDtypeStruct((layers, rows, width), BF16),
            jax.ShapeDtypeStruct((layers, cols, rows), BF16),
        ),
        in_specs=[pl.BlockSpec(memory_space=pltpu.SMEM), anywhere, anywhere, anywhere],
        out_specs=(anywhere, anywhere),
        scratch_shapes=scratch,
        compiler_params=pltpu.CompilerParams(
            collective_id=0, has_side_effects=True, vmem_limit_bytes=60 * 2**20
        ),
        name="refresh",
    )(owner, acts, prior, grads)
    return inverse, jnp.swapaxes(precond, 1, 2)


def solution(mesh):
    placed = (P(None, "dp", None), P("dp", "grad", None), P(), P(None, "grad", "dp"))
    return jax.shard_map(
        on_device,
        mesh=mesh,
        in_specs=placed,
        out_specs=(P(None, "grad", None), P(None, "grad", "dp")),
        check_vma=False,
    )
```

```python
import functools

import jax
import jax.numpy as jnp
from jax import lax
from jax.experimental import pallas as pl
from jax.experimental.pallas import tpu as pltpu
from jax.sharding import PartitionSpec as P

MESH = pl.DeviceIdType.MESH
BF16, F32 = jnp.bfloat16, jnp.float32
DAMPING = 0.001
NX, NY, NZ = 4, 4, 8
B = 128
SEMS = 128
CUT = 48


class Copies:
    def __init__(self, send, recv):
        self.send, self.recv, self.count, self.started = send, recv, 0, []

    def start(self, src, dst, device):
        copy = pltpu.make_async_remote_copy(
            src_ref=src,
            dst_ref=dst,
            send_sem=self.send.at[self.count],
            recv_sem=self.recv.at[self.count],
            device_id=device,
            device_id_type=MESH,
        )
        self.count += 1
        copy.start()
        self.started.append(copy)
        return copy

    def finish(self):
        for copy in self.started:
            copy.wait_send()


def add_rows(buf, rows, extras):
    start, size = rows
    tile = 80 if size % 80 == 0 else 64

    @pl.loop(0, size // tile)
    def _(i):
        at = pl.ds(pl.multiple_of(start + i * tile, 16), tile)
        total = buf[at, :].astype(F32)
        for ref, offset in extras:
            total += ref[pl.ds(pl.multiple_of(offset + i * tile, 16), tile), :].astype(F32)
        buf[at, :] = total.astype(BF16)


def ring_reduce(copies, buf, base, shard, n, me, nxt, prv, land):
    half, far = shard // 2, n // 2
    ways = ((0, 1, nxt), (1, -1, prv))

    def row(k, q):
        return base + lax.rem(me + k + n, n) * shard + q * half

    flying = {}
    for step in range(far + 1):
        k = far - step
        order = [(way, q) for q in (0, 1) for way in (0, 1)]
        order = sorted(order, key=lambda wq: wq[0] != wq[1])
        if k == 0:
            for q in (0, 1):
                for way in (0, 1):
                    flying.pop((way, q)).wait_recv()
                add_rows(buf, (row(0, q), half), [(land.at[way, far - 1], q * half) for way in (0, 1)])
            return
        for way, q in order:
            _, sign, device = ways[way]
            old = flying.pop((way, q), None)
            if old is not None:
                old.wait_recv()
                add_rows(buf, (row(sign * k, q), half), [(land.at[way, step - 1], q * half)])
            if step == 0 and way != q:
                continue
            flying[way, q] = copies.start(
                buf.at[pl.ds(pl.multiple_of(row(sign * k, q), 16), half)],
                land.at[way, step, pl.ds(q * half, half)],
                device,
            )
        yield


def direct_reduce(copies, buf, row, peers, land):
    flying = []
    for slot, (where, device) in enumerate(peers):
        source = buf.at[pl.ds(pl.multiple_of(row(*where), 16), 80)]
        flying.append(copies.start(source, land.at[slot], device))
    yield
    total = buf[pl.ds(pl.multiple_of(row(0, 0), 16), 80), :].astype(F32)
    for slot, copy in enumerate(flying):
        copy.wait_recv()
        total += land[slot].astype(F32)
    return total


def direct_gather(copies, block, devices):
    flying = [copies.start(block, block, device) for device in devices]
    yield
    for copy in flying:
        copy.wait_recv()


def ring_gather(copies, part, n, me, nxt, prv):
    far = n // 2
    ways = ((0, 1, nxt), (1, -1, prv))
    flying = {}
    for step in range(far + 1):
        order = [(way, p) for p in (0, 1) for way in (0, 1)]
        order = sorted(order, key=lambda wp: wp[0] != wp[1])
        for way, p in order:
            _, sign, device = ways[way]
            old = flying.pop((way, p), None)
            if old is not None:
                old.wait_recv()
            if step == far or (step == far - 1 and way != p):
                continue
            block = part(p, lax.rem(me - sign * step + n, n))
            flying[way, p] = copies.start(block, block, device)
        if step < far:
            yield


def in_order(*chains):
    for chain in chains:
        next(chain, None)


def matmul_tiles(rows, cols, body):
    tm, tn = 768, 512
    tm = min(tm, rows)

    @pl.loop(0, rows // tm)
    def _(i):
        @pl.loop(0, cols // tn)
        def _(j):
            body(pl.multiple_of(i * tm, tm), tm, pl.ds(pl.multiple_of(j * tn, tn), tn))


def kernel(
    owner, acts, prior, grads, inverse, precond,
    acts_v, prior_v, gram_p, prior_p, land_gz, land_g, land_px, land_p,
    all_a, all_x, full_a, full_x, prod, iter1, second, so_far, inv_v, grads_v, pre_v,
    send, recv, local,
):
    tokens, width = acts.shape[1], acts.shape[2]
    total = tokens * lax.axis_size("dp")
    dp, g = lax.axis_index("dp"), lax.axis_index("grad")
    x, z, yh = lax.rem(dp, NX), lax.rem(dp // NX, NZ), dp // (NX * NZ)
    h, c = g // 2, lax.rem(g, 2)
    y = yh * 2 + h
    sib = 1 - c

    def at(dx=0, dy=0, dz=0, core=c):
        x2 = lax.rem(x + dx + NX, NX)
        y2 = lax.rem(y + dy + NY, NY)
        z2 = lax.rem(z + dz + NZ, NZ)
        return ((y2 // 2) * (NZ * NX) + z2 * NX + x2, lax.rem(y2, 2) * 2 + core)

    xn, xp, zn, zp = at(dx=1), at(dx=-1), at(dz=1), at(dz=-1)
    yn, yp = at(dy=1), at(dy=-1)
    xs = [at(dx=k) for k in range(1, NX)]
    ys = [at(dy=k) for k in range(1, NY)]
    zs = [at(dz=k) for k in range(1, NZ)]
    xys = [at(dx=i, dy=j) for i in range(NX) for j in range(NY) if i or j]
    gram_peers = [((i, j), at(dx=i, dy=2 * j)) for i in range(NX) for j in range(2) if i or j]
    prior_peers = [((i, j), at(dz=i, dy=2 * j)) for i in range(NZ) for j in range(2) if i or j]
    sibling = at(core=sib)
    partner, across = (dp, (1 - h) * 2 + c), (dp, (1 - h) * 2 + sib)
    rows = prior.shape[1]

    loads = [
        pltpu.make_async_copy(prior.at[0], prior_v.at[pl.ds(pl.multiple_of(c * rows, 16), rows)], local.at[0]),
        pltpu.make_async_copy(acts.at[c], acts_v.at[:, pl.ds(0, width)], local.at[1]),
        pltpu.make_async_copy(
            acts.at[c, :, pl.ds(0, width // 2)], acts_v.at[:, pl.ds(width, width // 2)], local.at[2]
        ),
        pltpu.make_async_copy(
            grads.at[c], grads_v.at[:, pl.ds(pl.multiple_of(g * rows, 128), rows)], local.at[3]
        ),
    ]
    for load in loads:
        load.start()

    barrier = pltpu.get_barrier_semaphore()
    peers = [xn, at(dx=2), xp, *ys, zn, zp, sibling, across]
    for peer in peers:
        pl.semaphore_signal(barrier, inc=1, device_id=peer, device_id_type=MESH)
    pl.semaphore_wait(barrier, len(peers))

    copies = Copies(send, recv)
    mine = pl.ds(pl.multiple_of(c * rows, 16), rows)
    swap = copies.start(prior.at[0], prior_v.at[mine], sibling)
    place = pl.ds(pl.multiple_of(g * rows, 128), rows)
    grad_copies = [
        copies.start(grads.at[sib], grads_v.at[:, place], sibling),
        copies.start(grads.at[c], grads_v.at[:, place], partner),
        copies.start(grads.at[sib], grads_v.at[:, place], across),
    ]

    for load in loads:
        load.wait()

    def block_rows(p):
        return pl.ds(pl.multiple_of(p * B, B), B)

    dims = (((0,), (0,)), ((), ()))

    @pl.loop(0, 6)
    def _(ii):
        i = 6 * h + ii
        left = acts_v[:, pl.ds(pl.multiple_of(i * B, B), B)]
        right = acts_v[:, pl.ds(pl.multiple_of(i * B, B), 6 * B)]
        part = lax.dot_general(left, right, dims, preferred_element_type=F32).astype(BF16)
        for d in range(6):
            gram_p[block_rows(ii * 6 + d), :] = part[:, d * B : (d + 1) * B]

    @pl.loop(0, 3)
    def _(e):
        i = 9 * h + e
        j = lax.rem(i + 6, 12)
        left = acts_v[:, pl.ds(pl.multiple_of(i * B, B), B)]
        right = acts_v[:, pl.ds(pl.multiple_of(j * B, B), B)]
        part = lax.dot_general(left, right, dims, preferred_element_type=F32).astype(BF16)
        gram_p[block_rows(36 + e), :] = part

    gram_p[block_rows(39), :] = jnp.zeros((B, B), BF16)

    def reduce_gram():
        yield from ring_reduce(copies, gram_p, 0, 640, NZ, z, zn, zp, land_gz)

        def row(i, j):
            return z * 640 + lax.rem(x + i, NX) * 160 + lax.rem(yh + j, 2) * 80

        summed = yield from direct_reduce(copies, gram_p, row, gram_peers, land_g)
        at_row = row(0, 0) + lax.broadcasted_iota(jnp.int32, (80, B), 0)
        lane = lax.broadcasted_iota(jnp.int32, (80, B), 1)
        on_diag = lane == at_row
        for p in range(6, 36, 6):
            on_diag = on_diag | (lane + p * B == at_row)
        value = summed / total
        value = jnp.where(on_diag, value + DAMPING, value)
        all_a[h, z, x, yh] = value.astype(BF16)

    def reduce_prior():
        yield from ring_reduce(copies, prior_p, 0, 1280, NX, x, xn, xp, land_px)
        yield

        def row(i, j):
            return x * 1280 + lax.rem(z + i, NZ) * 160 + lax.rem(yh + j, 2) * 80

        summed = yield from direct_reduce(copies, prior_p, row, prior_peers, land_p)
        all_x[h, x, z, yh] = summed.astype(BF16)

    first, rest = pl.ds(0, CUT), pl.ds(CUT, 80 - CUT)

    def gather_a_z():
        yield from direct_gather(copies, all_a.at[h, z, x, yh, first], xys)
        yield from ring_gather(
            copies, lambda p, k: all_a.at[p, k, :, :, first], NZ, z, zn, zp
        )

    def gather_a_y():
        yield from direct_gather(copies, all_a.at[h, z, x, yh, rest], zs)
        yield from direct_gather(copies, all_a.at[h, :, x, yh, rest], xs)
        yield from ring_gather(
            copies,
            lambda p, k: all_a.at[lax.rem(k, 2), pl.ds(p * 4, 4), :, k // 2, rest],
            NY, y, yn, yp,
        )

    def gather_x_x():
        yield from direct_gather(copies, all_x.at[h, x, z, yh, first], zs)
        yield from direct_gather(copies, all_x.at[h, x, :, yh, first], ys)
        yield from ring_gather(
            copies, lambda p, k: all_x.at[p, k, :, :, first], NX, x, xn, xp
        )

    def gather_x_y():
        yield from direct_gather(copies, all_x.at[h, x, z, yh, rest], zs)
        yield from direct_gather(copies, all_x.at[h, x, :, yh, rest], xs)
        yield from ring_gather(
            copies,
            lambda p, k: all_x.at[lax.rem(k, 2), :, pl.ds(p * 4, 4), k // 2, rest],
            NY, y, yn, yp,
        )

    def prior_chain():
        swap.wait_recv()
        keep = jnp.where(owner[c] == dp, 1.0, 0.0).astype(F32)

        def pack(p, i, j):
            block = prior_v[
                pl.ds(pl.multiple_of((i - 6 * h) * B, B), B), pl.ds(pl.multiple_of(j * B, B), B)
            ]
            prior_p[block_rows(p), :] = (block.astype(F32) * keep).astype(BF16)

        @pl.loop(0, 6)
        def _(ii):
            for d in range(6):
                i = 6 * h + ii
                pack(ii * 6 + d, i, lax.rem(i + d, 12))

        @pl.loop(0, 3)
        def _(e):
            i = 9 * h + e
            pack(36 + e, i, lax.rem(i + 6, 12))

        prior_p[block_rows(39), :] = jnp.zeros((B, B), BF16)
        yield from reduce_prior()

    def unpack(packed, full, groups):
        @pl.loop(0, 2)
        def _(half):
            for group in range(groups):
                size = 40 // groups
                value = packed[half, group].reshape(size * B, B)
                for b in range(size):
                    p = group * size + b
                    if p == 39:
                        continue
                    i, d = (6 * half + p // 6, p % 6) if p < 36 else (9 * half + p - 36, 6)
                    j = lax.rem(i + d, 12)
                    block = value[b * B : (b + 1) * B]
                    full[block_rows(i), block_rows(j)] = block
                    if d:
                        full[block_rows(j), block_rows(i)] = block.T

    gram, fetched = reduce_gram(), prior_chain()
    in_order(gram, fetched, gram, fetched, gram, fetched, gram, gram, fetched, gram)
    a_z, a_y, x_x, x_y = gather_a_z(), gather_a_y(), gather_x_x(), gather_x_y()
    in_order(a_z, a_y, fetched, x_x, x_y)
    in_order(a_z, x_x, a_y, x_y)
    in_order(a_z, x_x, a_y, x_y)
    in_order(a_z, a_z, x_x, a_y, x_y)
    in_order(x_x, x_y)
    unpack(all_x, full_x, NX)
    in_order(a_y, a_z)
    unpack(all_a, full_a, NZ)

    first_row = h * 2 * rows

    def find_product(r, tm, cols):
        at_rows = pl.ds(r, tm)
        prod[at_rows, cols] = jnp.dot(
            full_a[at_rows, :], full_x[:, cols], preferred_element_type=F32
        ).astype(BF16)

    def first_iterate(r, tm, cols):
        source = pl.ds(pl.multiple_of(first_row + r, 16), tm)
        squared = jnp.dot(full_x[source, :], prod[:, cols], preferred_element_type=F32)
        iter1[pl.ds(r, tm), cols] = (2.0 * full_x[source, cols].astype(F32) - squared).astype(BF16)

    def find_second(r, tm, cols):
        at_rows = pl.ds(r, tm)
        value = jnp.dot(iter1[at_rows, :], prod[:, cols], preferred_element_type=F32)
        second[at_rows, cols] = value.astype(BF16)
        so_far[at_rows, cols] = 2.0 * (iter1[at_rows, cols].astype(F32) - value)

    def last_iterate(start):
        def body(r, tm, cols):
            at_rows = pl.ds(pl.multiple_of(start + r, 16), tm)
            value = jnp.dot(second[at_rows, :], prod[:, cols], preferred_element_type=F32)
            inv_v[at_rows, cols] = (so_far[at_rows, cols] + value).astype(BF16)

        return body

    def precondition(start):
        value = lax.dot_general(
            grads_v[...],
            inv_v[pl.ds(pl.multiple_of(start, 16), rows), :],
            (((1,), (1,)), ((), ())),
            preferred_element_type=F32,
        )
        pre_v[:, pl.ds(pl.multiple_of(start, 128), rows)] = value.astype(BF16)

    matmul_tiles(width, width, find_product)
    matmul_tiles(2 * rows, width, first_iterate)
    matmul_tiles(2 * rows, width, find_second)
    matmul_tiles(rows, width, last_iterate(sib * rows))
    theirs = pl.ds(pl.multiple_of(sib * rows, 16), rows)
    their_cols = pl.ds(pl.multiple_of(sib * rows, 128), rows)
    my_cols = pl.ds(pl.multiple_of(c * rows, 128), rows)
    results = [copies.start(inv_v.at[theirs], inverse.at[c], sibling)]
    for copy in grad_copies:
        copy.wait_recv()
    precondition(sib * rows)
    results.append(copies.start(pre_v.at[:, their_cols], precond.at[c], sibling))
    matmul_tiles(rows, width, last_iterate(c * rows))
    stores = [pltpu.make_async_copy(inv_v.at[mine], inverse.at[c], local.at[0])]
    stores[0].start()
    precondition(c * rows)
    stores.append(pltpu.make_async_copy(pre_v.at[:, my_cols], precond.at[c], local.at[1]))
    stores[1].start()
    for store in stores:
        store.wait()
    for copy in results:
        copy.wait_recv()
    copies.finish()


def on_device(acts, prior, owner, grads):
    layers, tokens, width = acts.shape
    rows, cols = prior.shape[1], grads.shape[2]
    grads = jnp.swapaxes(grads, 1, 2)
    anywhere = pl.BlockSpec(memory_space=pl.ANY)
    packed = 40 * B
    scratch = [
        pltpu.VMEM((tokens, width + width // 2), BF16),
        pltpu.VMEM((2 * rows, width), BF16),
        pltpu.VMEM((packed, B), BF16),
        pltpu.VMEM((packed, B), BF16),
        pltpu.VMEM((2, 4, 640, B), BF16),
        pltpu.VMEM((7, 80, B), BF16),
        pltpu.VMEM((2, 2, 1280, B), BF16),
        pltpu.VMEM((15, 80, B), BF16),
        pltpu.VMEM((2, NZ, NX, 2, 80, B), BF16),
        pltpu.VMEM((2, NX, NZ, 2, 80, B), BF16),
        pltpu.VMEM((width, width), BF16),
        pltpu.VMEM((width, width), BF16),
        pltpu.VMEM((width, width), BF16),
        pltpu.VMEM((2 * rows, width), BF16),
        pltpu.VMEM((2 * rows, width), BF16),
        pltpu.VMEM((2 * rows, width), F32),
        pltpu.VMEM((2 * rows, width), BF16),
        pltpu.VMEM((cols, 4 * rows), BF16),
        pltpu.VMEM((cols, 2 * rows), BF16),
        pltpu.SemaphoreType.DMA((SEMS,)),
        pltpu.SemaphoreType.DMA((SEMS,)),
        pltpu.SemaphoreType.DMA((4,)),
    ]
    inverse, precond = pl.pallas_call(
        kernel,
        out_shape=(
            jax.ShapeDtypeStruct((layers, rows, width), BF16),
            jax.ShapeDtypeStruct((layers, cols, rows), BF16),
        ),
        in_specs=[pl.BlockSpec(memory_space=pltpu.SMEM), anywhere, anywhere, anywhere],
        out_specs=(anywhere, anywhere),
        scratch_shapes=scratch,
        compiler_params=pltpu.CompilerParams(
            collective_id=0, has_side_effects=True, vmem_limit_bytes=60 * 2**20
        ),
        name="refresh",
    )(owner, acts, prior, grads)
    return inverse, jnp.swapaxes(precond, 1, 2)


def solution(mesh):
    placed = (P(None, "dp", None), P("dp", "grad", None), P(), P(None, "grad", "dp"))
    return jax.shard_map(
        on_device,
        mesh=mesh,
        in_specs=placed,
        out_specs=(P(None, "grad", None), P(None, "grad", "dp")),
        check_vma=False,
    )
```

```python
import functools

import jax
import jax.numpy as jnp
from jax import lax
from jax.experimental import pallas as pl
from jax.experimental.pallas import tpu as pltpu
from jax.sharding import PartitionSpec as P

MESH = pl.DeviceIdType.MESH
BF16, F32 = jnp.bfloat16, jnp.float32
DAMPING = 0.001
NX, NY, NZ = 4, 4, 8
B = 128
SEMS = 128
CUT_A, CUT_X = 48, 48


class Copies:
    def __init__(self, send, recv):
        self.send, self.recv, self.count, self.started = send, recv, 0, []

    def start(self, src, dst, device):
        copy = pltpu.make_async_remote_copy(
            src_ref=src,
            dst_ref=dst,
            send_sem=self.send.at[self.count],
            recv_sem=self.recv.at[self.count],
            device_id=device,
            device_id_type=MESH,
        )
        self.count += 1
        copy.start()
        self.started.append(copy)
        return copy

    def finish(self):
        for copy in self.started:
            copy.wait_send()


def add_rows(buf, rows, extras):
    start, size = rows
    tile = 80 if size % 80 == 0 else 64

    @pl.loop(0, size // tile)
    def _(i):
        at = pl.ds(pl.multiple_of(start + i * tile, 16), tile)
        total = buf[at, :].astype(F32)
        for ref, offset in extras:
            total += ref[pl.ds(pl.multiple_of(offset + i * tile, 16), tile), :].astype(F32)
        buf[at, :] = total.astype(BF16)


def ring_reduce(copies, buf, base, shard, n, me, nxt, prv, land):
    half, far = shard // 2, n // 2
    ways = ((0, 1, nxt), (1, -1, prv))

    def row(k, q):
        return base + lax.rem(me + k + n, n) * shard + q * half

    flying = {}
    for step in range(far + 1):
        k = far - step
        order = [(way, q) for q in (0, 1) for way in (0, 1)]
        order = sorted(order, key=lambda wq: wq[0] != wq[1])
        if k == 0:
            for q in (0, 1):
                for way in (0, 1):
                    flying.pop((way, q)).wait_recv()
                add_rows(buf, (row(0, q), half), [(land.at[way, far - 1], q * half) for way in (0, 1)])
            return
        for way, q in order:
            _, sign, device = ways[way]
            old = flying.pop((way, q), None)
            if old is not None:
                old.wait_recv()
                add_rows(buf, (row(sign * k, q), half), [(land.at[way, step - 1], q * half)])
            if step == 0 and way != q:
                continue
            flying[way, q] = copies.start(
                buf.at[pl.ds(pl.multiple_of(row(sign * k, q), 16), half)],
                land.at[way, step, pl.ds(q * half, half)],
                device,
            )
        yield


def direct_reduce(copies, buf, row, peers, land):
    flying = []
    for slot, (where, device) in enumerate(peers):
        source = buf.at[pl.ds(pl.multiple_of(row(*where), 16), 80)]
        flying.append(copies.start(source, land.at[slot], device))
    yield
    total = buf[pl.ds(pl.multiple_of(row(0, 0), 16), 80), :].astype(F32)
    for slot, copy in enumerate(flying):
        copy.wait_recv()
        total += land[slot].astype(F32)
    return total


def direct_gather(copies, block, devices):
    flying = [copies.start(block, block, device) for device in devices]
    yield
    for copy in flying:
        copy.wait_recv()


def ring_gather(copies, part, n, me, nxt, prv):
    far = n // 2
    ways = ((0, 1, nxt), (1, -1, prv))
    flying = {}
    for step in range(far + 1):
        order = [(way, p) for p in (0, 1) for way in (0, 1)]
        order = sorted(order, key=lambda wp: wp[0] != wp[1])
        for way, p in order:
            _, sign, device = ways[way]
            old = flying.pop((way, p), None)
            if old is not None:
                old.wait_recv()
            if step == far or (step == far - 1 and way != p):
                continue
            block = part(p, lax.rem(me - sign * step + n, n))
            flying[way, p] = copies.start(block, block, device)
        if step < far:
            yield


def in_order(*chains):
    for chain in chains:
        next(chain, None)


def matmul_tiles(rows, cols, body):
    tm, tn = 768, 512
    tm = min(tm, rows)

    @pl.loop(0, rows // tm)
    def _(i):
        @pl.loop(0, cols // tn)
        def _(j):
            body(pl.multiple_of(i * tm, tm), tm, pl.ds(pl.multiple_of(j * tn, tn), tn))


def kernel(
    owner, acts, prior, grads, inverse, precond,
    acts_v, prior_v, gram_p, prior_p, land_gz, land_g, land_px, land_py, land_p,
    all_a, all_x, full_a, full_x, prod, iter1, second, so_far, inv_v, grads_v, pre_v,
    send, recv, local,
):
    tokens, width = acts.shape[1], acts.shape[2]
    total = tokens * lax.axis_size("dp")
    dp, g = lax.axis_index("dp"), lax.axis_index("grad")
    x, z, yh = lax.rem(dp, NX), lax.rem(dp // NX, NZ), dp // (NX * NZ)
    h, c = g // 2, lax.rem(g, 2)
    y = yh * 2 + h
    sib = 1 - c

    def at(dx=0, dy=0, dz=0, core=c):
        x2 = lax.rem(x + dx + NX, NX)
        y2 = lax.rem(y + dy + NY, NY)
        z2 = lax.rem(z + dz + NZ, NZ)
        return ((y2 // 2) * (NZ * NX) + z2 * NX + x2, lax.rem(y2, 2) * 2 + core)

    xn, xp, zn, zp = at(dx=1), at(dx=-1), at(dz=1), at(dz=-1)
    yn, yp = at(dy=1), at(dy=-1)
    xs = [at(dx=k) for k in range(1, NX)]
    ys = [at(dy=k) for k in range(1, NY)]
    zs = [at(dz=k) for k in range(1, NZ)]
    xys = [at(dx=i, dy=j) for i in range(NX) for j in range(NY) if i or j]
    gram_peers = [((i, j), at(dx=i, dy=2 * j)) for i in range(NX) for j in range(2) if i or j]
    prior_peers = [((i, 0), at(dz=i)) for i in range(1, NZ)]
    sibling = at(core=sib)
    partner, across = (dp, (1 - h) * 2 + c), (dp, (1 - h) * 2 + sib)
    rows = prior.shape[1]

    loads = [
        pltpu.make_async_copy(prior.at[0], prior_v.at[pl.ds(pl.multiple_of(c * rows, 16), rows)], local.at[0]),
        pltpu.make_async_copy(acts.at[c], acts_v.at[:, pl.ds(0, width)], local.at[1]),
        pltpu.make_async_copy(
            acts.at[c, :, pl.ds(0, width // 2)], acts_v.at[:, pl.ds(width, width // 2)], local.at[2]
        ),
        pltpu.make_async_copy(
            grads.at[c], grads_v.at[:, pl.ds(pl.multiple_of(g * rows, 128), rows)], local.at[3]
        ),
    ]
    for load in loads:
        load.start()

    barrier = pltpu.get_barrier_semaphore()
    peers = [xn, at(dx=2), xp, *ys, zn, at(dz=4), zp, sibling, across]
    for peer in peers:
        pl.semaphore_signal(barrier, inc=1, device_id=peer, device_id_type=MESH)

    for load in loads:
        load.wait()

    def block_rows(p):
        return pl.ds(pl.multiple_of(p * B, B), B)

    dims = (((0,), (0,)), ((), ()))

    @pl.loop(0, 6)
    def _(ii):
        i = 6 * h + ii
        left = acts_v[:, pl.ds(pl.multiple_of(i * B, B), B)]
        right = acts_v[:, pl.ds(pl.multiple_of(i * B, B), 6 * B)]
        part = lax.dot_general(left, right, dims, preferred_element_type=F32).astype(BF16)
        for d in range(6):
            gram_p[block_rows(ii * 6 + d), :] = part[:, d * B : (d + 1) * B]

    @pl.loop(0, 3)
    def _(e):
        i = 9 * h + e
        j = lax.rem(i + 6, 12)
        left = acts_v[:, pl.ds(pl.multiple_of(i * B, B), B)]
        right = acts_v[:, pl.ds(pl.multiple_of(j * B, B), B)]
        part = lax.dot_general(left, right, dims, preferred_element_type=F32).astype(BF16)
        gram_p[block_rows(36 + e), :] = part

    gram_p[block_rows(39), :] = jnp.zeros((B, B), BF16)

    pl.semaphore_wait(barrier, len(peers))

    copies = Copies(send, recv)
    mine = pl.ds(pl.multiple_of(c * rows, 16), rows)
    swap = copies.start(prior.at[0], prior_v.at[mine], sibling)
    place = pl.ds(pl.multiple_of(g * rows, 128), rows)
    grad_copies = [
        copies.start(grads.at[sib], grads_v.at[:, place], sibling),
        copies.start(grads.at[c], grads_v.at[:, place], partner),
        copies.start(grads.at[sib], grads_v.at[:, place], across),
    ]

    def reduce_gram():
        yield from ring_reduce(copies, gram_p, 0, 640, NZ, z, zn, zp, land_gz)

        def row(i, j):
            return z * 640 + lax.rem(x + i, NX) * 160 + lax.rem(yh + j, 2) * 80

        summed = yield from direct_reduce(copies, gram_p, row, gram_peers, land_g)
        at_row = row(0, 0) + lax.broadcasted_iota(jnp.int32, (80, B), 0)
        lane = lax.broadcasted_iota(jnp.int32, (80, B), 1)
        on_diag = lane == at_row
        for p in range(6, 36, 6):
            on_diag = on_diag | (lane + p * B == at_row)
        value = summed / total
        value = jnp.where(on_diag, value + DAMPING, value)
        all_a[h, z, x, yh] = value.astype(BF16)

    def reduce_prior():
        yield from ring_reduce(copies, prior_p, 0, 1280, NX, x, xn, xp, land_px)
        other = pl.ds(pl.multiple_of(x * 1280 + (1 - yh) * 640, 16), 640)
        mine_now = x * 1280 + yh * 640
        across_y = copies.start(prior_p.at[other], land_py, at(dy=2))
        yield
        across_y.wait_recv()
        add_rows(prior_p, (mine_now, 640), [(land_py, 0)])

        def row(i, j):
            return mine_now + lax.rem(z + i, NZ) * 80

        summed = yield from direct_reduce(copies, prior_p, row, prior_peers, land_p)
        all_x[h, x, yh, z] = summed.astype(BF16)

    first, rest = pl.ds(0, CUT_A), pl.ds(CUT_A, 80 - CUT_A)
    first_x, rest_x = pl.ds(0, CUT_X), pl.ds(CUT_X, 80 - CUT_X)

    def gather_a_z():
        yield from direct_gather(copies, all_a.at[h, z, x, yh, first], xys)
        yield from ring_gather(
            copies, lambda p, k: all_a.at[p, k, :, :, first], NZ, z, zn, zp
        )

    def gather_a_y():
        yield from direct_gather(copies, all_a.at[h, z, x, yh, rest], zs)
        yield from direct_gather(copies, all_a.at[h, :, x, yh, rest], xs)
        yield from ring_gather(
            copies,
            lambda p, k: all_a.at[lax.rem(k, 2), pl.ds(p * 4, 4), :, k // 2, rest],
            NY, y, yn, yp,
        )

    def gather_x_x():
        yield from direct_gather(copies, all_x.at[h, x, yh, z, first_x], zs)
        yield from direct_gather(copies, all_x.at[h, x, yh, :, first_x], ys)
        yield from ring_gather(
            copies, lambda p, k: all_x.at[p, k, :, :, first_x], NX, x, xn, xp
        )

    def gather_x_y():
        yield from direct_gather(copies, all_x.at[h, x, yh, z, rest_x], zs)
        yield from direct_gather(copies, all_x.at[h, x, yh, :, rest_x], xs)
        yield from ring_gather(
            copies,
            lambda p, k: all_x.at[lax.rem(k, 2), :, k // 2, pl.ds(p * 4, 4), rest_x],
            NY, y, yn, yp,
        )

    def prior_chain():
        swap.wait_recv()
        keep = jnp.where(owner[c] == dp, 1.0, 0.0).astype(F32)

        def pack(p, i, j):
            block = prior_v[
                pl.ds(pl.multiple_of((i - 6 * h) * B, B), B), pl.ds(pl.multiple_of(j * B, B), B)
            ]
            prior_p[block_rows(p), :] = (block.astype(F32) * keep).astype(BF16)

        @pl.loop(0, 6)
        def _(ii):
            for d in range(6):
                i = 6 * h + ii
                pack(ii * 6 + d, i, lax.rem(i + d, 12))

        @pl.loop(0, 3)
        def _(e):
            i = 9 * h + e
            pack(36 + e, i, lax.rem(i + 6, 12))

        prior_p[block_rows(39), :] = jnp.zeros((B, B), BF16)
        yield from reduce_prior()

    def unpack(packed, full, groups):
        @pl.loop(0, 2)
        def _(half):
            for group in range(groups):
                size = 40 // groups
                value = packed[half, group].reshape(size * B, B)
                for b in range(size):
                    p = group * size + b
                    if p == 39:
                        continue
                    i, d = (6 * half + p // 6, p % 6) if p < 36 else (9 * half + p - 36, 6)
                    j = lax.rem(i + d, 12)
                    block = value[b * B : (b + 1) * B]
                    full[block_rows(i), block_rows(j)] = block
                    if d:
                        full[block_rows(j), block_rows(i)] = block.T

    gram, fetched = reduce_gram(), prior_chain()
    a_z, a_y, x_x, x_y = gather_a_z(), gather_a_y(), gather_x_x(), gather_x_y()
    in_order(gram, fetched, gram, fetched, gram, fetched, gram, fetched, gram, fetched)
    in_order(x_x, x_y, gram, a_z, a_y, x_x, x_y)
    in_order(a_z, a_y, x_y, x_x, a_z, a_y, x_y)
    in_order(a_z, x_x, a_z, a_y)
    in_order(x_x, x_y)
    unpack(all_x, full_x, NX)
    in_order(a_y, a_z)
    unpack(all_a, full_a, NZ)

    first_row = h * 2 * rows

    def find_product(r, tm, cols):
        at_rows = pl.ds(r, tm)
        prod[at_rows, cols] = jnp.dot(
            full_a[at_rows, :], full_x[:, cols], preferred_element_type=F32
        ).astype(BF16)

    def first_iterate(r, tm, cols):
        source = pl.ds(pl.multiple_of(first_row + r, 16), tm)
        squared = jnp.dot(full_x[source, :], prod[:, cols], preferred_element_type=F32)
        iter1[pl.ds(r, tm), cols] = (2.0 * full_x[source, cols].astype(F32) - squared).astype(BF16)

    def find_second(r, tm, cols):
        at_rows = pl.ds(r, tm)
        value = jnp.dot(iter1[at_rows, :], prod[:, cols], preferred_element_type=F32)
        second[at_rows, cols] = value.astype(BF16)
        so_far[at_rows, cols] = 2.0 * (iter1[at_rows, cols].astype(F32) - value)

    def last_iterate(start, result):
        def body(r, tm, cols):
            at_rows = pl.ds(pl.multiple_of(start + r, 16), tm)
            value = jnp.dot(second[at_rows, :], prod[:, cols], preferred_element_type=F32)
            result[pl.ds(r, tm), cols] = (so_far[at_rows, cols] + value).astype(BF16)

        return body

    def precondition(result):
        return lax.dot_general(
            grads_v[...], result[...], (((1,), (1,)), ((), ())), preferred_element_type=F32
        ).astype(BF16)

    matmul_tiles(width, width, find_product)
    matmul_tiles(2 * rows, width, first_iterate)
    matmul_tiles(2 * rows, width, find_second)
    matmul_tiles(rows, width, last_iterate(sib * rows, inv_v))
    results = [copies.start(inv_v, inverse.at[c], sibling)]
    for copy in grad_copies:
        copy.wait_recv()
    pre_v[...] = precondition(inv_v)
    results.append(copies.start(pre_v, precond.at[c], sibling))
    matmul_tiles(rows, width, last_iterate(c * rows, inverse.at[c]))
    precond[c] = precondition(inverse.at[c])
    for copy in results:
        copy.wait_recv()
    copies.finish()


def on_device(acts, prior, owner, grads):
    layers, tokens, width = acts.shape
    rows, cols = prior.shape[1], grads.shape[2]
    grads = jnp.swapaxes(grads, 1, 2)
    anywhere = pl.BlockSpec(memory_space=pl.ANY)
    packed = 40 * B
    scratch = [
        pltpu.VMEM((tokens, width + width // 2), BF16),
        pltpu.VMEM((2 * rows, width), BF16),
        pltpu.VMEM((packed, B), BF16),
        pltpu.VMEM((packed, B), BF16),
        pltpu.VMEM((2, 4, 640, B), BF16),
        pltpu.VMEM((7, 80, B), BF16),
        pltpu.VMEM((2, 2, 1280, B), BF16),
        pltpu.VMEM((640, B), BF16),
        pltpu.VMEM((7, 80, B), BF16),
        pltpu.VMEM((2, NZ, NX, 2, 80, B), BF16),
        pltpu.VMEM((2, NX, 2, NZ, 80, B), BF16),
        pltpu.VMEM((width, width), BF16),
        pltpu.VMEM((width, width), BF16),
        pltpu.VMEM((width, width), BF16),
        pltpu.VMEM((2 * rows, width), BF16),
        pltpu.VMEM((2 * rows, width), BF16),
        pltpu.VMEM((2 * rows, width), F32),
        pltpu.VMEM((rows, width), BF16),
        pltpu.VMEM((cols, 4 * rows), BF16),
        pltpu.VMEM((cols, rows), BF16),
        pltpu.SemaphoreType.DMA((SEMS,)),
        pltpu.SemaphoreType.DMA((SEMS,)),
        pltpu.SemaphoreType.DMA((4,)),
    ]
    inverse, precond = pl.pallas_call(
        kernel,
        out_shape=(
            pltpu.VMEM((layers, rows, width), BF16),
            pltpu.VMEM((layers, cols, rows), BF16),
        ),
        in_specs=[pl.BlockSpec(memory_space=pltpu.SMEM), anywhere, anywhere, anywhere],
        out_specs=(pl.BlockSpec(memory_space=pltpu.VMEM),) * 2,
        scratch_shapes=scratch,
        compiler_params=pltpu.CompilerParams(
            collective_id=0, has_side_effects=True, vmem_limit_bytes=60 * 2**20
        ),
        name="refresh",
    )(owner, acts, prior, grads)
    return inverse, jnp.swapaxes(precond, 1, 2)


def solution(mesh):
    placed = (P(None, "dp", None), P("dp", "grad", None), P(), P(None, "grad", "dp"))
    return jax.shard_map(
        on_device,
        mesh=mesh,
        in_specs=placed,
        out_specs=(P(None, "grad", None), P(None, "grad", "dp")),
        check_vma=False,
    )
```
